512 devices in a mesh: pipe: 16 (over z_lo, core), dp: 32 (over z_hi, y, x).
Axes of the slice: x: 4, y: 4, z: 16 (z_hi: 2, z_lo: 8; z = z_hi * 8 + z_lo), core: 2. Of those that a mesh axis runs over, the one named last changes fastest.
Arguments:
- queries: bfloat16 [16, 4096, 4096], P('pipe', 'dp'), may hold values from -8 to 8
- keys: bfloat16 [16, 4096, 512], P('pipe', 'dp'), may hold values from -8 to 8
- values: bfloat16 [16, 4096, 512], P('pipe', 'dp'), may hold values from -8 to 8
- block_pairs: int32 [16, 256, 2], P('pipe'), may hold values from 0 to 31, as said below
Outputs:
- attended: bfloat16 [16, 4096, 4096], P('pipe', 'dp')
The draws below stay inside these ranges and needn't reach their ends.
Inputs may be any that keep to these rules, and one draw needn't show every extreme that they name: `block_pairs`: for each section, entries j * 8 to (j + 1) * 8 - 1 hold the pairs of query tile j (first element j); their key tiles are distinct and the first of them is j.
All inputs are finite; a program needn't handle non-finite values.
Results may differ from the reference program's by a relative error of at most 0.0047.
Values may be sent and summed in bfloat16 or wider, within the bound.
No kernel may reach another device: no remote copies, remote signals or barrier semaphores. Data moves between devices by JAX's collectives and lax.ppermute only.
A program may use at most 64 MiB of HBM per device.

```python
import math
import jax
import jax.numpy as jnp
from jax import lax

TILE_TOKENS = 128
QUERY_HEADS = 32
KEY_VALUE_HEADS = 4
HEAD_SIZE = 128
KEY_TILES_READ = 8
RELAY_SECTIONS = 16
MICRO_TOKENS = 4096
QBLOCKS = 32
PAIRS = 256


def draw_queries(key, part):
    key = jax.random.fold_in(key, 11)
    base_scores = jnp.clip(jax.random.normal(key, (RELAY_SECTIONS, MICRO_TOKENS, QUERY_HEADS * HEAD_SIZE), jnp.float32), -8.0, 8.0)
    return base_scores.astype(jnp.bfloat16)


def draw_keys(key, part):
    key = jax.random.fold_in(key, 12)
    base_scores = jnp.clip(jax.random.normal(key, (RELAY_SECTIONS, MICRO_TOKENS, KEY_VALUE_HEADS * HEAD_SIZE), jnp.float32), -8.0, 8.0)
    return base_scores.astype(jnp.bfloat16)


def draw_values(key, part):
    key = jax.random.fold_in(key, 13)
    base_scores = jnp.clip(jax.random.normal(key, (RELAY_SECTIONS, MICRO_TOKENS, KEY_VALUE_HEADS * HEAD_SIZE), jnp.float32), -8.0, 8.0)
    return base_scores.astype(jnp.bfloat16)


def draw_block_pairs(key, part):
    key = jax.random.fold_in(key, 14)
    column = jnp.arange(QBLOCKS, dtype=jnp.int32)
    scores = jax.random.randint(key, (RELAY_SECTIONS, QBLOCKS, QBLOCKS), 0, 1 << 16, jnp.int32) * QBLOCKS + column[None, None, :]
    diagonal = column[:, None] == column[None, :]
    scores = jnp.where(diagonal[None], (1 << 16) * QBLOCKS + QBLOCKS, scores)
    _, chosen_tiles = lax.top_k(scores, KEY_TILES_READ)
    rows = jnp.broadcast_to(column[None, :, None], (RELAY_SECTIONS, QBLOCKS, KEY_TILES_READ))
    pairs = jnp.stack((rows, chosen_tiles.astype(jnp.int32)), axis=-1)
    return pairs.reshape(RELAY_SECTIONS, PAIRS, 2).astype(jnp.int32)


def setup_inputs(seed: int = 0) -> dict:
    key_of = jax.random.split(jax.random.key(seed), 5)
    return {
        "queries": draw_queries(jax.random.fold_in(key_of[4], 71), 0),
        "keys": draw_keys(jax.random.fold_in(key_of[4], 71), 0),
        "values": draw_values(jax.random.fold_in(key_of[4], 71), 0),
        "block_pairs": draw_block_pairs(jax.random.fold_in(key_of[4], 71), 0),
    }


def attend(queries_t, keys_t, values_t):
    scale = 1.0 / math.sqrt(HEAD_SIZE)
    scores = jnp.einsum('brd,bld->brl', queries_t.astype(jnp.float32), keys_t.astype(jnp.float32)) * scale
    largest = lax.optimization_barrier(jnp.max(scores, axis=-1, keepdims=True))
    weights = jnp.exp(scores - largest)
    total = lax.optimization_barrier(jnp.sum(weights, axis=-1, keepdims=True))
    rounded = weights.astype(jnp.bfloat16)
    mixed_rows = jnp.einsum('brl,bld->brd', rounded.astype(jnp.float32), values_t.astype(jnp.float32))
    return (mixed_rows / total).astype(jnp.bfloat16)

def section_rows(operands):
    query_section_rows, key_section_rows, value_section_rows, pairs = operands
    tile_blocks = MICRO_TOKENS // TILE_TOKENS
    head_group = QUERY_HEADS // KEY_VALUE_HEADS
    chosen_tiles = pairs[:, 1].reshape(tile_blocks, KEY_TILES_READ).astype(jnp.int32)
    query_tile_rows = query_section_rows.reshape(tile_blocks, TILE_TOKENS, KEY_VALUE_HEADS, head_group, HEAD_SIZE)
    key_tile_rows = key_section_rows.reshape(tile_blocks, TILE_TOKENS, KEY_VALUE_HEADS, HEAD_SIZE)
    value_tile_rows = value_section_rows.reshape(tile_blocks, TILE_TOKENS, KEY_VALUE_HEADS, HEAD_SIZE)

    def one_block(pieces):
        query_tile_block, picked_indices = pieces
        key_tile_block = jnp.take(key_tile_rows, picked_indices, axis=0).reshape(KEY_TILES_READ * TILE_TOKENS, KEY_VALUE_HEADS, HEAD_SIZE).transpose(1, 0, 2)
        value_tile_block = jnp.take(value_tile_rows, picked_indices, axis=0).reshape(KEY_TILES_READ * TILE_TOKENS, KEY_VALUE_HEADS, HEAD_SIZE).transpose(1, 0, 2)
        query_head_rows = query_tile_block.transpose(1, 0, 2, 3).reshape(KEY_VALUE_HEADS, TILE_TOKENS * head_group, HEAD_SIZE)
        mixed_rows = attend(query_head_rows, key_tile_block, value_tile_block)
        return mixed_rows.reshape(KEY_VALUE_HEADS, TILE_TOKENS, head_group, HEAD_SIZE).transpose(1, 0, 2, 3).reshape(TILE_TOKENS, QUERY_HEADS * HEAD_SIZE)
    return lax.map(one_block, (query_tile_rows, chosen_tiles)).reshape(MICRO_TOKENS, QUERY_HEADS * HEAD_SIZE)

def reference(queries, keys, values, block_pairs):
    q_in = jnp.roll(queries, 1, axis=0)
    k_in = jnp.roll(keys, 1, axis=0)
    v_in = jnp.roll(values, 1, axis=0)
    return lax.map(section_rows, (q_in, k_in, v_in, block_pairs))
```

```python
import math

import jax
import jax.numpy as jnp
from jax import lax
from jax.experimental import pallas as pl
from jax.experimental.pallas import tpu as pltpu
from jax.sharding import PartitionSpec as P

TILE = 128
HEADS = 4
GROUP = 8
HEAD_SIZE = 128
PICKS = 8
WIDE = GROUP * HEAD_SIZE
SECTIONS = 16
SIDE = 4
PLANE = SIDE * SIDE
TILES = 2 * PLANE
AXES = ("pipe", "dp")
SCALE = math.log2(math.e) / math.sqrt(HEAD_SIZE)


def relayed(swap, turn):
    pairs = []
    for section in range(SECTIONS):
        for tile in range(TILES):
            half, row, column = tile // PLANE, tile // SIDE % SIDE, tile % SIDE
            target = (half ^ swap) * PLANE + (row + turn) % SIDE * SIDE + column
            pairs.append((section * TILES + tile, (section + 1) % SECTIONS * TILES + target))
    return pairs


def attention_kernel(slots, places, *refs):
    query_refs, kv_ref, out_ref = refs[:SIDE], refs[SIDE], refs[SIDE + 1]
    k_sel, v_sel = refs[SIDE + 2], refs[SIDE + 3]
    for turn in range(SIDE):
        for pick in range(PICKS):
            slot = slots[turn * PICKS + pick]
            rows = pl.ds(pick * TILE, TILE)
            k_sel[rows, :] = kv_ref[slot, :, :HEAD_SIZE]
            v_sel[rows, :] = kv_ref[slot, :, HEAD_SIZE:]
        for head in range(GROUP):
            columns = pl.ds(head * HEAD_SIZE, HEAD_SIZE)
            scores = lax.dot_general(
                query_refs[turn][:, columns], k_sel[...], (((1,), (1,)), ((), ())),
                preferred_element_type=jnp.float32,
            )
            largest = jnp.max(scores, axis=-1, keepdims=True)
            weights = jnp.exp2((scores - largest) * SCALE)
            total = jnp.sum(weights, axis=-1, keepdims=True)
            mixed = jnp.dot(
                weights.astype(jnp.bfloat16), v_sel[...], preferred_element_type=jnp.float32
            )
            out_ref[places[turn], :, columns] = (mixed / total).astype(jnp.bfloat16)


def attention(slots, places, queries, kv):
    vmem = pl.BlockSpec(memory_space=pltpu.VMEM)
    smem = pl.BlockSpec(memory_space=pltpu.SMEM)
    return pl.pallas_call(
        attention_kernel,
        out_shape=jax.ShapeDtypeStruct((SIDE, TILE, WIDE), jnp.bfloat16),
        in_specs=[smem, smem] + [vmem] * (SIDE + 1),
        out_specs=vmem,
        scratch_shapes=[
            pltpu.VMEM((PICKS * TILE, HEAD_SIZE), jnp.bfloat16),
            pltpu.VMEM((PICKS * TILE, HEAD_SIZE), jnp.bfloat16),
        ],
        compiler_params=pltpu.CompilerParams(vmem_limit_bytes=32 * 1024 * 1024),
        cost_estimate=pl.CostEstimate(
            flops=2 * 2 * SIDE * GROUP * TILE * PICKS * TILE * HEAD_SIZE,
            bytes_accessed=4 * 1024 * 1024,
            transcendentals=SIDE * GROUP * TILE * PICKS * TILE,
        ),
    )(slots, places, *queries, kv)


def on_device(queries, keys, values, block_pairs):
    queries, keys, values = queries[0], keys[0], values[0]
    place = lax.axis_index("dp")
    half, row, column = place // PLANE, place // SIDE % SIDE, place % SIDE
    groups_row = [[h * PLANE + y * SIDE + x for y in range(SIDE)] for h in range(2) for x in range(SIDE)]
    groups_plane = [[h * PLANE + i for i in range(PLANE)] for h in range(2)]

    def head_columns(array, head):
        return array[:, head * HEAD_SIZE : (head + 1) * HEAD_SIZE]

    kv = jnp.stack(
        [
            jnp.concatenate([head_columns(keys, h), head_columns(values, h)], axis=1)
            for h in range(HEADS)
        ]
    )
    far = lax.ppermute(kv, AXES, relayed(1, 0))
    near = lax.ppermute(kv, AXES, relayed(0, 0))
    pieces = [
        lax.ppermute(
            lax.dynamic_slice_in_dim(queries, (row + turn) % SIDE * WIDE, WIDE, 1),
            AXES,
            relayed(0, turn),
        )
        for turn in range(SIDE)
    ]
    both = jnp.stack([near, far], axis=1)
    sent = jnp.broadcast_to(both[:, None], (HEADS, SIDE) + both.shape[1:])
    sent = sent.reshape((PLANE, 2, TILE, 2 * HEAD_SIZE))
    landed = lax.all_to_all(sent, "dp", 0, 0, axis_index_groups=groups_plane)
    landed = landed.reshape(PLANE * 2, TILE, 2 * HEAD_SIZE)

    places = (row - jnp.arange(SIDE, dtype=jnp.int32)) % SIDE
    blocks = half * PLANE + places * SIDE + column
    chosen = jnp.take(block_pairs[0, :, 1].reshape(TILES, PICKS), blocks, axis=0)
    slots = (chosen % PLANE) * 2 + ((chosen // PLANE) ^ half)
    mixed = attention(slots.reshape(-1).astype(jnp.int32), places, pieces, landed)
    back = lax.all_to_all(mixed, "dp", 0, 0, axis_index_groups=groups_row)
    return jnp.concatenate([back[h] for h in range(HEADS)], axis=1)[None]


def solution(mesh):
    placed = (
        P("pipe", "dp", None),
        P("pipe", "dp", None),
        P("pipe", "dp", None),
        P("pipe", None, None),
    )
    return jax.shard_map(
        on_device, mesh=mesh, in_specs=placed, out_specs=P("pipe", "dp", None), check_vma=False
    )
```

```python
import math

import jax
import jax.numpy as jnp
from jax import lax
from jax.experimental import pallas as pl
from jax.experimental.pallas import tpu as pltpu
from jax.sharding import PartitionSpec as P

TILE = 128
HEADS = 4
GROUP = 8
HEAD_SIZE = 128
PICKS = 8
WIDE = GROUP * HEAD_SIZE
SECTIONS = 16
SIDE = 4
PLANE = SIDE * SIDE
TILES = 2 * PLANE
AXES = ("pipe", "dp")
SCALE = math.log2(math.e) / math.sqrt(HEAD_SIZE)
VMEM = pl.BlockSpec(memory_space=pltpu.VMEM)
SMEM = pl.BlockSpec(memory_space=pltpu.SMEM)


def route(step, swap, turn):
    pairs = []
    for section in range(SECTIONS):
        for tile in range(TILES):
            half, row, column = tile // PLANE, tile // SIDE % SIDE, tile % SIDE
            target = (half ^ swap) * PLANE + (row + turn) % SIDE * SIDE + column
            pairs.append((section * TILES + tile, (section + step) % SECTIONS * TILES + target))
    return pairs


def attention_kernel(slots, query_ref, near_ref, far_ref, out_ref, k_sel, v_sel):
    for pick in range(PICKS):
        slot = slots[pick]
        rows = pl.ds(pick * TILE, TILE)
        for side, held in enumerate((near_ref, far_ref)):

            @pl.when(slot // PLANE == side)
            def _():
                k_sel[rows, :] = held[slot % PLANE, :, :HEAD_SIZE]
                v_sel[rows, :] = held[slot % PLANE, :, HEAD_SIZE:]

    for head in range(GROUP):
        columns = pl.ds(head * HEAD_SIZE, HEAD_SIZE)
        scores = lax.dot_general(
            query_ref[:, columns], k_sel[...], (((1,), (1,)), ((), ())),
            preferred_element_type=jnp.float32,
        )
        largest = jnp.max(scores, axis=-1, keepdims=True)
        weights = jnp.exp2((scores - largest) * SCALE)
        total = jnp.sum(weights, axis=-1, keepdims=True)
        mixed = jnp.dot(
            weights.astype(jnp.bfloat16), v_sel[...], preferred_element_type=jnp.float32
        )
        out_ref[:, columns] = (mixed / total).astype(jnp.bfloat16)


def attention(slots, queries, near, far):
    return pl.pallas_call(
        attention_kernel,
        out_shape=jax.ShapeDtypeStruct((TILE, WIDE), jnp.bfloat16),
        in_specs=[SMEM, VMEM, VMEM, VMEM],
        out_specs=VMEM,
        scratch_shapes=[
            pltpu.VMEM((PICKS * TILE, HEAD_SIZE), jnp.bfloat16),
            pltpu.VMEM((PICKS * TILE, HEAD_SIZE), jnp.bfloat16),
        ],
        compiler_params=pltpu.CompilerParams(vmem_limit_bytes=32 * 1024 * 1024),
        cost_estimate=pl.CostEstimate(
            flops=2 * 2 * GROUP * TILE * PICKS * TILE * HEAD_SIZE,
            bytes_accessed=1024 * 1024,
            transcendentals=GROUP * TILE * PICKS * TILE,
        ),
    )(slots, queries, near, far)


def assemble_kernel(heads, *refs):
    for turn in range(SIDE):
        start = pl.multiple_of(heads[turn] * WIDE, WIDE)
        refs[SIDE][:, pl.ds(start, WIDE)] = refs[turn][...]


def assemble(heads, pieces):
    return pl.pallas_call(
        assemble_kernel,
        out_shape=jax.ShapeDtypeStruct((TILE, HEADS * WIDE), jnp.bfloat16),
        in_specs=[SMEM] + [VMEM] * SIDE,
        out_specs=VMEM,
        compiler_params=pltpu.CompilerParams(vmem_limit_bytes=16 * 1024 * 1024),
        cost_estimate=pl.CostEstimate(flops=0, bytes_accessed=2 * 1024 * 1024, transcendentals=0),
    )(heads, *pieces)


def on_device(queries, keys, values, block_pairs):
    queries, keys, values = queries[0], keys[0], values[0]
    place = lax.axis_index("dp")
    half, row, column = place // PLANE, place // SIDE % SIDE, place % SIDE
    groups = [[h * PLANE + i for i in range(PLANE)] for h in range(2)]

    def head_columns(array, head):
        return array[:, head * HEAD_SIZE : (head + 1) * HEAD_SIZE]

    def spread(held):
        sent = jnp.broadcast_to(held[:, None], (HEADS, SIDE) + held.shape[1:])
        sent = sent.reshape((PLANE,) + held.shape[1:])
        return lax.all_to_all(sent, "dp", 0, 0, axis_index_groups=groups)

    kv = jnp.stack(
        [
            jnp.concatenate([head_columns(keys, h), head_columns(values, h)], axis=1)
            for h in range(HEADS)
        ]
    )
    far = lax.ppermute(kv, AXES, route(0, 1, 0))
    near_landed = spread(kv)
    pairs = lax.ppermute(block_pairs[0, :, 1].reshape(TILES, PICKS), AXES, route(-1, 0, 0))
    heads = (row + jnp.arange(SIDE, dtype=jnp.int32)) % SIDE
    pieces = [lax.dynamic_slice_in_dim(queries, heads[turn] * WIDE, WIDE, 1) for turn in range(SIDE)]
    for turn in range(1, SIDE):
        pieces[turn] = lax.ppermute(pieces[turn], AXES, route(0, 0, turn))
    far, near_landed, pairs, *pieces = lax.optimization_barrier((far, near_landed, pairs, *pieces))
    far_landed = spread(far)

    blocks = half * PLANE + (row - jnp.arange(SIDE, dtype=jnp.int32)) % SIDE * SIDE + column
    chosen = jnp.take(pairs, blocks, axis=0)
    slots = (chosen % PLANE) + ((chosen // PLANE) ^ half) * PLANE
    back = [None] * SIDE
    for turn in (2, 1, 3, 0):
        mixed = attention(slots[turn], pieces[turn], near_landed, far_landed)
        back[turn] = lax.ppermute(mixed, AXES, route(1, 0, -turn))
    return assemble(heads, back)[None]


def solution(mesh):
    placed = (
        P("pipe", "dp", None),
        P("pipe", "dp", None),
        P("pipe", "dp", None),
        P("pipe", None, None),
    )
    return jax.shard_map(
        on_device, mesh=mesh, in_specs=placed, out_specs=P("pipe", "dp", None), check_vma=False
    )
```

```python
import math

import jax
import jax.numpy as jnp
from jax import lax
from jax.experimental import pallas as pl
from jax.experimental.pallas import tpu as pltpu
from jax.sharding import PartitionSpec as P

TILE = 128
HEADS = 4
GROUP = 8
HEAD_SIZE = 128
PICKS = 8
WIDE = GROUP * HEAD_SIZE
SECTIONS = 16
SIDE = 4
PLANE = SIDE * SIDE
TILES = 2 * PLANE
AXES = ("pipe", "dp")
SCALE = math.log2(math.e) / math.sqrt(HEAD_SIZE)
VMEM = pl.BlockSpec(memory_space=pltpu.VMEM)
SMEM = pl.BlockSpec(memory_space=pltpu.SMEM)


def route(step, swap, turn):
    pairs = []
    for section in range(SECTIONS):
        for tile in range(TILES):
            half, row, column = tile // PLANE, tile // SIDE % SIDE, tile % SIDE
            target = (half ^ swap) * PLANE + (row + turn) % SIDE * SIDE + column
            pairs.append((section * TILES + tile, (section + step) % SECTIONS * TILES + target))
    return pairs


def attention_kernel(slots, *refs):
    query_refs, near_ref, far_ref = refs[:SIDE], refs[SIDE], refs[SIDE + 1]
    out_refs, k_sel, v_sel = refs[SIDE + 2 : 2 * SIDE + 2], refs[-2], refs[-1]
    for turn in range(SIDE):
        attend(slots, turn, query_refs[turn], near_ref, far_ref, out_refs[turn], k_sel, v_sel)


def attend(slots, turn, query_ref, near_ref, far_ref, out_ref, k_sel, v_sel):
    for pick in range(PICKS):
        slot = slots[turn, pick]
        rows = pl.ds(pick * TILE, TILE)
        for side, held in enumerate((near_ref, far_ref)):

            @pl.when(slot // PLANE == side)
            def _():
                k_sel[rows, :] = held[slot % PLANE, :, :HEAD_SIZE]
                v_sel[rows, :HEAD_SIZE] = held[slot % PLANE, :, HEAD_SIZE:]

    v_sel[:, HEAD_SIZE:] = jnp.ones((PICKS * TILE, HEAD_SIZE), jnp.bfloat16)

    def scores_of(head):
        return lax.dot_general(
            query_ref[:, pl.ds(head * HEAD_SIZE, HEAD_SIZE)], k_sel[...], (((1,), (1,)), ((), ())),
            preferred_element_type=jnp.float32,
        )

    later = scores_of(0)
    for head in range(GROUP):
        scores = later
        if head + 1 < GROUP:
            later = scores_of(head + 1)
        largest = jnp.max(scores, axis=-1, keepdims=True)
        weights = jnp.exp2((scores - largest) * SCALE).astype(jnp.bfloat16)
        mixed = jnp.dot(weights, v_sel[...], preferred_element_type=jnp.float32)
        out_ref[:, pl.ds(head * HEAD_SIZE, HEAD_SIZE)] = (
            mixed[:, :HEAD_SIZE] / mixed[:, HEAD_SIZE:]
        ).astype(jnp.bfloat16)


def attention(slots, queries, near, far):
    return pl.pallas_call(
        attention_kernel,
        out_shape=[jax.ShapeDtypeStruct((TILE, WIDE), jnp.bfloat16)] * SIDE,
        in_specs=[SMEM] + [VMEM] * (SIDE + 2),
        out_specs=[VMEM] * SIDE,
        scratch_shapes=[
            pltpu.VMEM((PICKS * TILE, HEAD_SIZE), jnp.bfloat16),
            pltpu.VMEM((PICKS * TILE, 2 * HEAD_SIZE), jnp.bfloat16),
        ],
        compiler_params=pltpu.CompilerParams(vmem_limit_bytes=24 * 1024 * 1024),
        cost_estimate=pl.CostEstimate(
            flops=2 * 2 * SIDE * GROUP * TILE * PICKS * TILE * HEAD_SIZE,
            bytes_accessed=4 * 1024 * 1024,
            transcendentals=SIDE * GROUP * TILE * PICKS * TILE,
        ),
    )(slots, *queries, near, far)


def assemble_kernel(heads, *refs):
    pieces, out_ref, sems = refs[:SIDE], refs[SIDE], refs[SIDE + 1]
    copies = []
    for turn in range(SIDE):
        columns = pl.ds(pl.multiple_of(heads[turn] * WIDE, WIDE), WIDE)
        copies.append(pltpu.make_async_copy(pieces[turn], out_ref.at[:, columns], sems.at[turn]))
        copies[-1].start()
    for copy in copies:
        copy.wait()


def assemble(heads, pieces):
    return pl.pallas_call(
        assemble_kernel,
        out_shape=jax.ShapeDtypeStruct((TILE, HEADS * WIDE), jnp.bfloat16),
        in_specs=[SMEM] + [VMEM] * SIDE,
        out_specs=pl.BlockSpec(memory_space=pl.ANY),
        scratch_shapes=[pltpu.SemaphoreType.DMA((SIDE,))],
        compiler_params=pltpu.CompilerParams(vmem_limit_bytes=6 * 1024 * 1024),
        cost_estimate=pl.CostEstimate(flops=0, bytes_accessed=2 * 1024 * 1024, transcendentals=0),
    )(heads, *pieces)


def repeat_kernel(held_ref, sent_ref, sems):
    copies = []
    for slot in range(PLANE):
        copies.append(
            pltpu.make_async_copy(held_ref.at[slot // SIDE], sent_ref.at[slot], sems.at[slot])
        )
        copies[-1].start()
    for copy in copies:
        copy.wait()


def repeated(held, cost):
    return pl.pallas_call(
        repeat_kernel,
        out_shape=jax.ShapeDtypeStruct((PLANE,) + held.shape[1:], held.dtype),
        in_specs=[VMEM],
        out_specs=pl.BlockSpec(memory_space=pl.ANY),
        scratch_shapes=[pltpu.SemaphoreType.DMA((PLANE,))],
        compiler_params=pltpu.CompilerParams(vmem_limit_bytes=6 * 1024 * 1024),
        cost_estimate=pl.CostEstimate(flops=cost, bytes_accessed=1280 * 1024, transcendentals=0),
    )(held)


def on_device(queries, keys, values, block_pairs):
    queries, keys, values = queries[0], keys[0], values[0]
    place = lax.axis_index("dp")
    half, row, column = place // PLANE, place // SIDE % SIDE, place % SIDE
    groups = [[h * PLANE + i for i in range(PLANE)] for h in range(2)]

    def head_columns(array, head):
        return array[:, head * HEAD_SIZE : (head + 1) * HEAD_SIZE]

    def spread(sent):
        return lax.all_to_all(sent, "dp", 0, 0, axis_index_groups=groups)

    kv = jnp.stack(
        [
            jnp.concatenate([head_columns(keys, h), head_columns(values, h)], axis=1)
            for h in range(HEADS)
        ]
    )
    far = lax.ppermute(kv, AXES, route(0, 1, 0))
    near_landed = spread(repeated(kv, 0))
    pairs = lax.ppermute(block_pairs[0, :, 1].reshape(TILES, PICKS), AXES, route(-1, 0, 0))
    heads = (row + jnp.arange(SIDE, dtype=jnp.int32)) % SIDE
    pieces = [lax.dynamic_slice_in_dim(queries, heads[turn] * WIDE, WIDE, 1) for turn in range(SIDE)]
    for turn in range(1, SIDE):
        pieces[turn] = lax.ppermute(pieces[turn], AXES, route(0, 0, turn))
    far_sent = repeated(far, 2 * 10**10)
    far_sent, near_landed, pairs, *pieces = lax.optimization_barrier(
        (far_sent, near_landed, pairs, *pieces)
    )
    far_landed = spread(far_sent)

    blocks = half * PLANE + (row - jnp.arange(SIDE, dtype=jnp.int32)) % SIDE * SIDE + column
    chosen = jnp.take(pairs, blocks, axis=0)
    slots = (chosen % PLANE) + ((chosen // PLANE) ^ half) * PLANE
    mixed = attention(slots, pieces, near_landed, far_landed)
    back = [lax.ppermute(mixed[turn], AXES, route(1, 0, -turn)) for turn in range(SIDE)]
    return assemble(heads, back)[None]


def solution(mesh):
    placed = (
        P("pipe", "dp", None),
        P("pipe", "dp", None),
        P("pipe", "dp", None),
        P("pipe", None, None),
    )
    return jax.shard_map(
        on_device, mesh=mesh, in_specs=placed, out_specs=P("pipe", "dp", None), check_vma=False
    )
```

```python
import math

import jax
import jax.numpy as jnp
from jax import lax
from jax.experimental import pallas as pl
from jax.experimental.pallas import tpu as pltpu
from jax.sharding import PartitionSpec as P

TILE = 128
HEADS = 4
GROUP = 8
HEAD_SIZE = 128
PICKS = 8
WIDE = GROUP * HEAD_SIZE
SECTIONS = 16
SIDE = 4
PLANE = SIDE * SIDE
TILES = 2 * PLANE
AXES = ("pipe", "dp")
SCALE = math.log2(math.e) / math.sqrt(HEAD_SIZE)
VMEM = pl.BlockSpec(memory_space=pltpu.VMEM)
SMEM = pl.BlockSpec(memory_space=pltpu.SMEM)


def route(step, swap, turn):
    pairs = []
    for section in range(SECTIONS):
        for tile in range(TILES):
            half, row, column = tile // PLANE, tile // SIDE % SIDE, tile % SIDE
            target = (half ^ swap) * PLANE + (row + turn) % SIDE * SIDE + column
            pairs.append((section * TILES + tile, (section + step) % SECTIONS * TILES + target))
    return pairs


def attention_kernel(slots, *refs):
    query_refs, near_ref, far_ref = refs[:SIDE], refs[SIDE], refs[SIDE + 1]
    out_refs, k_sel, v_sel = refs[SIDE + 2 : 2 * SIDE + 2], refs[-2], refs[-1]
    for turn in range(SIDE):
        attend(slots, turn, query_refs[turn], near_ref, far_ref, out_refs[turn], k_sel, v_sel)


def attend(slots, turn, query_ref, near_ref, far_ref, out_ref, k_sel, v_sel):
    for pick in range(PICKS):
        slot = slots[turn, pick]
        rows = pl.ds(pick * TILE, TILE)
        tile = jnp.where(slot < PLANE, near_ref[slot % PLANE], far_ref[slot % PLANE])
        k_sel[rows, :] = tile[:, :HEAD_SIZE]
        v_sel[rows, :HEAD_SIZE] = tile[:, HEAD_SIZE:]

    v_sel[:, HEAD_SIZE:] = jnp.ones((PICKS * TILE, HEAD_SIZE), jnp.bfloat16)

    def scores_of(head):
        return lax.dot_general(
            query_ref[:, pl.ds(head * HEAD_SIZE, HEAD_SIZE)], k_sel[...], (((1,), (1,)), ((), ())),
            preferred_element_type=jnp.float32,
        )

    later = scores_of(0)
    for head in range(GROUP):
        scores = later
        if head + 1 < GROUP:
            later = scores_of(head + 1)
        largest = jnp.max(scores, axis=-1, keepdims=True)
        weights = jnp.exp2((scores - largest) * SCALE).astype(jnp.bfloat16)
        mixed = jnp.dot(weights, v_sel[...], preferred_element_type=jnp.float32)
        out_ref[:, pl.ds(head * HEAD_SIZE, HEAD_SIZE)] = (
            mixed[:, :HEAD_SIZE] / mixed[:, HEAD_SIZE:]
        ).astype(jnp.bfloat16)


def attention(slots, queries, near, far):
    return pl.pallas_call(
        attention_kernel,
        out_shape=[jax.ShapeDtypeStruct((TILE, WIDE), jnp.bfloat16)] * SIDE,
        in_specs=[SMEM] + [VMEM] * (SIDE + 2),
        out_specs=[VMEM] * SIDE,
        scratch_shapes=[
            pltpu.VMEM((PICKS * TILE, HEAD_SIZE), jnp.bfloat16),
            pltpu.VMEM((PICKS * TILE, 2 * HEAD_SIZE), jnp.bfloat16),
        ],
        compiler_params=pltpu.CompilerParams(vmem_limit_bytes=24 * 1024 * 1024),
        cost_estimate=pl.CostEstimate(
            flops=2 * 2 * SIDE * GROUP * TILE * PICKS * TILE * HEAD_SIZE,
            bytes_accessed=4 * 1024 * 1024,
            transcendentals=SIDE * GROUP * TILE * PICKS * TILE,
        ),
    )(slots, *queries, near, far)


def assemble_kernel(heads, *refs):
    pieces, out_ref, sems = refs[:SIDE], refs[SIDE], refs[SIDE + 1]
    copies = []
    for turn in range(SIDE):
        columns = pl.ds(pl.multiple_of(heads[turn] * WIDE, WIDE), WIDE)
        copies.append(pltpu.make_async_copy(pieces[turn], out_ref.at[:, columns], sems.at[turn]))
        copies[-1].start()
    for copy in copies:
        copy.wait()


def assemble(heads, pieces):
    return pl.pallas_call(
        assemble_kernel,
        out_shape=jax.ShapeDtypeStruct((TILE, HEADS * WIDE), jnp.bfloat16),
        in_specs=[SMEM] + [VMEM] * SIDE,
        out_specs=pl.BlockSpec(memory_space=pl.ANY),
        scratch_shapes=[pltpu.SemaphoreType.DMA((SIDE,))],
        compiler_params=pltpu.CompilerParams(vmem_limit_bytes=6 * 1024 * 1024),
        cost_estimate=pl.CostEstimate(flops=0, bytes_accessed=2 * 1024 * 1024, transcendentals=0),
    )(heads, *pieces)


def split_kernel(heads, queries_ref, *refs):
    copies = []
    for turn in range(SIDE):
        columns = pl.ds(pl.multiple_of(heads[turn] * WIDE, WIDE), WIDE)
        copies.append(
            pltpu.make_async_copy(queries_ref.at[:, columns], refs[turn], refs[SIDE].at[turn])
        )
        copies[-1].start()
    for copy in copies:
        copy.wait()


def split(heads, queries):
    return list(
        pl.pallas_call(
            split_kernel,
            out_shape=[jax.ShapeDtypeStruct((TILE, WIDE), jnp.bfloat16)] * SIDE,
            in_specs=[SMEM, pl.BlockSpec(memory_space=pl.ANY)],
            out_specs=[VMEM] * SIDE,
            scratch_shapes=[pltpu.SemaphoreType.DMA((SIDE,))],
            compiler_params=pltpu.CompilerParams(vmem_limit_bytes=6 * 1024 * 1024),
            cost_estimate=pl.CostEstimate(
                flops=0, bytes_accessed=2 * 1024 * 1024, transcendentals=0
            ),
        )(heads, queries)
    )


def repeat_kernel(held_ref, sent_ref, sems):
    copies = []
    for slot in range(PLANE):
        copies.append(
            pltpu.make_async_copy(held_ref.at[slot // SIDE], sent_ref.at[slot], sems.at[slot])
        )
        copies[-1].start()
    for copy in copies:
        copy.wait()


def repeated(held, cost):
    return pl.pallas_call(
        repeat_kernel,
        out_shape=jax.ShapeDtypeStruct((PLANE,) + held.shape[1:], held.dtype),
        in_specs=[VMEM],
        out_specs=pl.BlockSpec(memory_space=pl.ANY),
        scratch_shapes=[pltpu.SemaphoreType.DMA((PLANE,))],
        compiler_params=pltpu.CompilerParams(vmem_limit_bytes=6 * 1024 * 1024),
        cost_estimate=pl.CostEstimate(flops=cost, bytes_accessed=1280 * 1024, transcendentals=0),
    )(held)


def on_device(queries, keys, values, block_pairs):
    queries, keys, values = queries[0], keys[0], values[0]
    place = lax.axis_index("dp")
    half, row, column = place >> 4, (place >> 2) & 3, place & 3
    turns = jnp.arange(SIDE, dtype=jnp.int32)
    groups = [[h * PLANE + i for i in range(PLANE)] for h in range(2)]

    def head_columns(array, head):
        return array[:, head * HEAD_SIZE : (head + 1) * HEAD_SIZE]

    def spread(sent):
        return lax.all_to_all(sent, "dp", 0, 0, axis_index_groups=groups)

    kv = jnp.stack(
        [
            jnp.concatenate([head_columns(keys, h), head_columns(values, h)], axis=1)
            for h in range(HEADS)
        ]
    )
    far = lax.ppermute(kv, AXES, route(0, 1, 0))
    pairs = lax.ppermute(block_pairs[0, :, 1].reshape(TILES, PICKS), AXES, route(-1, 0, 0))
    heads = (row + turns) & 3
    kv, *pieces = lax.optimization_barrier((kv, *split(heads, queries)))
    near_landed = spread(repeated(kv, 0))
    for turn in range(1, SIDE):
        pieces[turn] = lax.ppermute(pieces[turn], AXES, route(0, 0, turn))
    far_sent = repeated(far, 2 * 10**10)
    far_sent, near_landed, pairs, pieces[1], pieces[3] = lax.optimization_barrier(
        (far_sent, near_landed, pairs, pieces[1], pieces[3])
    )
    far_landed = spread(far_sent)

    blocks = half * PLANE + ((row - turns) & 3) * SIDE + column
    chosen = jnp.take(pairs, blocks, axis=0)
    slots = (chosen & 15) + ((chosen >> 4) ^ half) * PLANE
    mixed = attention(slots, pieces, near_landed, far_landed)
    back = [lax.ppermute(mixed[turn], AXES, route(1, 0, -turn)) for turn in range(SIDE)]
    return assemble(heads, back)[None]


def solution(mesh):
    placed = (
        P("pipe", "dp", None),
        P("pipe", "dp", None),
        P("pipe", "dp", None),
        P("pipe", None, None),
    )
    return jax.shard_map(
        on_device, mesh=mesh, in_specs=placed, out_specs=P("pipe", "dp", None), check_vma=False
    )
```

```python
import functools
import math

import jax
import jax.numpy as jnp
from jax import lax
from jax.experimental import pallas as pl
from jax.experimental.pallas import tpu as pltpu
from jax.sharding import PartitionSpec as P

TILE = 128
HEADS = 4
GROUP = 8
HEAD_SIZE = 128
PICKS = 8
WIDE = GROUP * HEAD_SIZE
SECTIONS = 16
SIDE = 4
PLANE = SIDE * SIDE
TILES = 2 * PLANE
AXES = ("pipe", "dp")
SCALE = math.log2(math.e) / math.sqrt(HEAD_SIZE)
VMEM = pl.BlockSpec(memory_space=pltpu.VMEM)
SMEM = pl.BlockSpec(memory_space=pltpu.SMEM)


def route(step, swap, turn):
    pairs = []
    for section in range(SECTIONS):
        for tile in range(TILES):
            half, row, column = tile // PLANE, tile // SIDE % SIDE, tile % SIDE
            target = (half ^ swap) * PLANE + (row + turn) % SIDE * SIDE + column
            pairs.append((section * TILES + tile, (section + step) % SECTIONS * TILES + target))
    return pairs


def attention_kernel(turns, slots, *refs):
    count = len(turns)
    query_refs, near_ref, far_ref = refs[:count], refs[count], refs[count + 1]
    out_refs, k_sel, v_sel = refs[count + 2 : 2 * count + 2], refs[-2], refs[-1]
    for query_ref, out_ref, turn in zip(query_refs, out_refs, turns):
        attend(slots, turn, query_ref, near_ref, far_ref, out_ref, k_sel, v_sel)


def attend(slots, turn, query_ref, near_ref, far_ref, out_ref, k_sel, v_sel):
    for pick in range(PICKS):
        slot = slots[turn, pick]
        rows = pl.ds(pick * TILE, TILE)
        tile = jnp.where(slot < PLANE, near_ref[slot % PLANE], far_ref[slot % PLANE])
        k_sel[rows, :] = tile[:, :HEAD_SIZE]
        v_sel[rows, :HEAD_SIZE] = tile[:, HEAD_SIZE:]

    v_sel[:, HEAD_SIZE:] = jnp.ones((PICKS * TILE, HEAD_SIZE), jnp.bfloat16)

    def scores_of(head):
        return lax.dot_general(
            query_ref[:, pl.ds(head * HEAD_SIZE, HEAD_SIZE)], k_sel[...], (((1,), (1,)), ((), ())),
            preferred_element_type=jnp.float32,
        )

    later = scores_of(0)
    for head in range(GROUP):
        scores = later
        if head + 1 < GROUP:
            later = scores_of(head + 1)
        largest = jnp.max(scores, axis=-1, keepdims=True)
        weights = jnp.exp2((scores - largest) * SCALE).astype(jnp.bfloat16)
        mixed = jnp.dot(weights, v_sel[...], preferred_element_type=jnp.float32)
        out_ref[:, pl.ds(head * HEAD_SIZE, HEAD_SIZE)] = (
            mixed[:, :HEAD_SIZE] / mixed[:, HEAD_SIZE:]
        ).astype(jnp.bfloat16)


def attention(turns, slots, queries, near, far):
    count = len(turns)
    return pl.pallas_call(
        functools.partial(attention_kernel, turns),
        out_shape=[jax.ShapeDtypeStruct((TILE, WIDE), jnp.bfloat16)] * count,
        in_specs=[SMEM] + [VMEM] * (count + 2),
        out_specs=[VMEM] * count,
        scratch_shapes=[
            pltpu.VMEM((PICKS * TILE, HEAD_SIZE), jnp.bfloat16),
            pltpu.VMEM((PICKS * TILE, 2 * HEAD_SIZE), jnp.bfloat16),
        ],
        compiler_params=pltpu.CompilerParams(vmem_limit_bytes=24 * 1024 * 1024),
        cost_estimate=pl.CostEstimate(
            flops=2 * 2 * count * GROUP * TILE * PICKS * TILE * HEAD_SIZE,
            bytes_accessed=count * 1024 * 1024,
            transcendentals=count * GROUP * TILE * PICKS * TILE,
        ),
    )(slots, *queries, near, far)


def assemble_kernel(heads, *refs):
    pieces, out_ref, sems = refs[:SIDE], refs[SIDE], refs[SIDE + 1]
    copies = []
    for turn in range(SIDE):
        columns = pl.ds(pl.multiple_of(heads[turn] * WIDE, WIDE), WIDE)
        copies.append(pltpu.make_async_copy(pieces[turn], out_ref.at[:, columns], sems.at[turn]))
        copies[-1].start()
    for copy in copies:
        copy.wait()


def assemble(heads, pieces):
    return pl.pallas_call(
        assemble_kernel,
        out_shape=jax.ShapeDtypeStruct((TILE, HEADS * WIDE), jnp.bfloat16),
        in_specs=[SMEM] + [VMEM] * SIDE,
        out_specs=pl.BlockSpec(memory_space=pl.ANY),
        scratch_shapes=[pltpu.SemaphoreType.DMA((SIDE,))],
        compiler_params=pltpu.CompilerParams(vmem_limit_bytes=6 * 1024 * 1024),
        cost_estimate=pl.CostEstimate(flops=0, bytes_accessed=2 * 1024 * 1024, transcendentals=0),
    )(heads, *pieces)


def split_kernel(heads, queries_ref, *refs):
    copies = []
    for turn in range(SIDE):
        columns = pl.ds(pl.multiple_of(heads[turn] * WIDE, WIDE), WIDE)
        copies.append(
            pltpu.make_async_copy(queries_ref.at[:, columns], refs[turn], refs[SIDE].at[turn])
        )
        copies[-1].start()
    for copy in copies:
        copy.wait()


def split(heads, queries):
    return list(
        pl.pallas_call(
            split_kernel,
            out_shape=[jax.ShapeDtypeStruct((TILE, WIDE), jnp.bfloat16)] * SIDE,
            in_specs=[SMEM, pl.BlockSpec(memory_space=pl.ANY)],
            out_specs=[VMEM] * SIDE,
            scratch_shapes=[pltpu.SemaphoreType.DMA((SIDE,))],
            compiler_params=pltpu.CompilerParams(vmem_limit_bytes=6 * 1024 * 1024),
            cost_estimate=pl.CostEstimate(
                flops=0, bytes_accessed=2 * 1024 * 1024, transcendentals=0
            ),
        )(heads, queries)
    )


def repeat_kernel(held_ref, sent_ref, sems):
    copies = []
    for slot in range(PLANE):
        copies.append(
            pltpu.make_async_copy(held_ref.at[slot // SIDE], sent_ref.at[slot], sems.at[slot])
        )
        copies[-1].start()
    for copy in copies:
        copy.wait()


def repeated(held, cost):
    return pl.pallas_call(
        repeat_kernel,
        out_shape=jax.ShapeDtypeStruct((PLANE,) + held.shape[1:], held.dtype),
        in_specs=[VMEM],
        out_specs=pl.BlockSpec(memory_space=pl.ANY),
        scratch_shapes=[pltpu.SemaphoreType.DMA((PLANE,))],
        compiler_params=pltpu.CompilerParams(vmem_limit_bytes=6 * 1024 * 1024),
        cost_estimate=pl.CostEstimate(flops=cost, bytes_accessed=1280 * 1024, transcendentals=0),
    )(held)


def on_device(queries, keys, values, block_pairs):
    queries, keys, values = queries[0], keys[0], values[0]
    place = lax.axis_index("dp")
    half, row, column = place >> 4, (place >> 2) & 3, place & 3
    steps = jnp.arange(SIDE, dtype=jnp.int32)
    groups = [[h * PLANE + i for i in range(PLANE)] for h in range(2)]

    def head_columns(array, head):
        return array[:, head * HEAD_SIZE : (head + 1) * HEAD_SIZE]

    def spread(sent):
        return lax.all_to_all(sent, "dp", 0, 0, axis_index_groups=groups)

    kv = jnp.stack(
        [
            jnp.concatenate([head_columns(keys, h), head_columns(values, h)], axis=1)
            for h in range(HEADS)
        ]
    )
    far = lax.ppermute(kv, AXES, route(0, 1, 0))
    pairs = lax.ppermute(block_pairs[0, :, 1].reshape(TILES, PICKS), AXES, route(-1, 0, 0))
    heads = (row + steps) & 3
    kv, *pieces = lax.optimization_barrier((kv, *split(heads, queries)))
    near_landed = spread(repeated(kv, 0))
    for turn in range(1, SIDE):
        pieces[turn] = lax.ppermute(pieces[turn], AXES, route(0, 0, turn))
    far_sent = repeated(far, 2 * 10**10)
    far_sent, near_landed, pairs, pieces[1], pieces[3] = lax.optimization_barrier(
        (far_sent, near_landed, pairs, pieces[1], pieces[3])
    )
    far_landed = spread(far_sent)

    blocks = half * PLANE + ((row - steps) & 3) * SIDE + column
    chosen = jnp.take(pairs, blocks, axis=0)
    slots = (chosen & 15) + ((chosen >> 4) ^ half) * PLANE
    back = [None] * SIDE
    for turns in ((1, 3), (2, 0)):
        mixed = attention(turns, slots, [pieces[turn] for turn in turns], near_landed, far_landed)
        for turn, rows in zip(turns, mixed):
            back[turn] = lax.ppermute(rows, AXES, route(1, 0, -turn))
        slots, mixed = lax.optimization_barrier((slots, mixed))
    return assemble(heads, back)[None]


def solution(mesh):
    placed = (
        P("pipe", "dp", None),
        P("pipe", "dp", None),
        P("pipe", "dp", None),
        P("pipe", None, None),
    )
    return jax.shard_map(
        on_device, mesh=mesh, in_specs=placed, out_specs=P("pipe", "dp", None), check_vma=False
    )
```

```python
import functools
import math

import jax
import jax.numpy as jnp
from jax import lax
from jax.experimental import pallas as pl
from jax.experimental.pallas import tpu as pltpu
from jax.sharding import PartitionSpec as P

TILE = 128
HEADS = 4
GROUP = 8
HEAD_SIZE = 128
PICKS = 8
WIDE = GROUP * HEAD_SIZE
SECTIONS = 16
SIDE = 4
PLANE = SIDE * SIDE
TILES = 2 * PLANE
AXES = ("pipe", "dp")
SCALE = math.log2(math.e) / math.sqrt(HEAD_SIZE)
VMEM = pl.BlockSpec(memory_space=pltpu.VMEM)
SMEM = pl.BlockSpec(memory_space=pltpu.SMEM)


def route(step, swap, turn):
    pairs = []
    for section in range(SECTIONS):
        for tile in range(TILES):
            half, row, column = tile // PLANE, tile // SIDE % SIDE, tile % SIDE
            target = (half ^ swap) * PLANE + (row + turn) % SIDE * SIDE + column
            pairs.append((section * TILES + tile, (section + step) % SECTIONS * TILES + target))
    return pairs


def attention_kernel(turns, slots, *refs):
    count = len(turns)
    query_refs, near_ref, far_ref = refs[:count], refs[count], refs[count + 1]
    out_refs, k_sel, v_sel = refs[count + 2 : 2 * count + 2], refs[-2], refs[-1]
    for query_ref, out_ref, turn in zip(query_refs, out_refs, turns):
        attend(slots, turn, query_ref, near_ref, far_ref, out_ref, k_sel, v_sel)


def attend(slots, turn, query_ref, near_ref, far_ref, out_ref, k_sel, v_sel):
    for pick in range(PICKS):
        slot = slots[turn, pick]
        rows = pl.ds(pick * TILE, TILE)
        tile = jnp.where(slot < PLANE, near_ref[slot % PLANE], far_ref[slot % PLANE])
        k_sel[rows, :] = tile[:, :HEAD_SIZE]
        v_sel[rows, :HEAD_SIZE] = tile[:, HEAD_SIZE:]

    v_sel[:, HEAD_SIZE:] = jnp.ones((PICKS * TILE, HEAD_SIZE), jnp.bfloat16)

    def scores_of(head):
        return lax.dot_general(
            query_ref[:, pl.ds(head * HEAD_SIZE, HEAD_SIZE)], k_sel[...], (((1,), (1,)), ((), ())),
            preferred_element_type=jnp.float32,
        )

    later = scores_of(0)
    for head in range(GROUP):
        scores = later
        if head + 1 < GROUP:
            later = scores_of(head + 1)
        largest = jnp.max(scores, axis=-1, keepdims=True)
        weights = jnp.exp2((scores - largest) * SCALE).astype(jnp.bfloat16)
        mixed = jnp.dot(weights, v_sel[...], preferred_element_type=jnp.float32)
        out_ref[:, pl.ds(head * HEAD_SIZE, HEAD_SIZE)] = (
            mixed[:, :HEAD_SIZE] / mixed[:, HEAD_SIZE:]
        ).astype(jnp.bfloat16)


def attention(turns, slots, queries, near, far):
    count = len(turns)
    return pl.pallas_call(
        functools.partial(attention_kernel, turns),
        out_shape=[jax.ShapeDtypeStruct((TILE, WIDE), jnp.bfloat16)] * count,
        in_specs=[SMEM] + [VMEM] * (count + 2),
        out_specs=[VMEM] * count,
        scratch_shapes=[
            pltpu.VMEM((PICKS * TILE, HEAD_SIZE), jnp.bfloat16),
            pltpu.VMEM((PICKS * TILE, 2 * HEAD_SIZE), jnp.bfloat16),
        ],
        compiler_params=pltpu.CompilerParams(vmem_limit_bytes=24 * 1024 * 1024),
        cost_estimate=pl.CostEstimate(
            flops=2 * 2 * count * GROUP * TILE * PICKS * TILE * HEAD_SIZE,
            bytes_accessed=count * 1024 * 1024,
            transcendentals=count * GROUP * TILE * PICKS * TILE,
        ),
    )(slots, *queries, near, far)


def assemble_kernel(heads, *refs):
    pieces, out_ref, sems = refs[:SIDE], refs[SIDE], refs[SIDE + 1]
    copies = []
    for turn in range(SIDE):
        columns = pl.ds(pl.multiple_of(heads[turn] * WIDE, WIDE), WIDE)
        copies.append(pltpu.make_async_copy(pieces[turn], out_ref.at[:, columns], sems.at[turn]))
        copies[-1].start()
    for copy in copies:
        copy.wait()


def assemble(heads, pieces):
    return pl.pallas_call(
        assemble_kernel,
        out_shape=jax.ShapeDtypeStruct((TILE, HEADS * WIDE), jnp.bfloat16),
        in_specs=[SMEM] + [VMEM] * SIDE,
        out_specs=pl.BlockSpec(memory_space=pl.ANY),
        scratch_shapes=[pltpu.SemaphoreType.DMA((SIDE,))],
        compiler_params=pltpu.CompilerParams(vmem_limit_bytes=6 * 1024 * 1024),
        cost_estimate=pl.CostEstimate(flops=0, bytes_accessed=2 * 1024 * 1024, transcendentals=0),
    )(heads, *pieces)


def split_kernel(heads, queries_ref, *refs):
    copies = []
    for turn in range(SIDE):
        columns = pl.ds(pl.multiple_of(heads[turn] * WIDE, WIDE), WIDE)
        copies.append(
            pltpu.make_async_copy(queries_ref.at[:, columns], refs[turn], refs[SIDE].at[turn])
        )
        copies[-1].start()
    for copy in copies:
        copy.wait()


def split(heads, queries):
    return list(
        pl.pallas_call(
            split_kernel,
            out_shape=[jax.ShapeDtypeStruct((TILE, WIDE), jnp.bfloat16)] * SIDE,
            in_specs=[SMEM, pl.BlockSpec(memory_space=pl.ANY)],
            out_specs=[VMEM] * SIDE,
            scratch_shapes=[pltpu.SemaphoreType.DMA((SIDE,))],
            compiler_params=pltpu.CompilerParams(vmem_limit_bytes=6 * 1024 * 1024),
            cost_estimate=pl.CostEstimate(
                flops=0, bytes_accessed=2 * 1024 * 1024, transcendentals=0
            ),
        )(heads, queries)
    )


def repeat_kernel(held_ref, sent_ref, sems):
    copies = []
    for slot in range(PLANE):
        copies.append(
            pltpu.make_async_copy(held_ref.at[slot // SIDE], sent_ref.at[slot], sems.at[slot])
        )
        copies[-1].start()
    for copy in copies:
        copy.wait()


def repeated(held, cost):
    return pl.pallas_call(
        repeat_kernel,
        out_shape=jax.ShapeDtypeStruct((PLANE,) + held.shape[1:], held.dtype),
        in_specs=[VMEM],
        out_specs=pl.BlockSpec(memory_space=pl.ANY),
        scratch_shapes=[pltpu.SemaphoreType.DMA((PLANE,))],
        compiler_params=pltpu.CompilerParams(vmem_limit_bytes=6 * 1024 * 1024),
        cost_estimate=pl.CostEstimate(flops=cost, bytes_accessed=1280 * 1024, transcendentals=0),
    )(held)


def on_device(queries, keys, values, block_pairs):
    queries, keys, values = queries[0], keys[0], values[0]
    place = lax.axis_index("dp")
    half, row, column = place >> 4, (place >> 2) & 3, place & 3
    steps = jnp.arange(SIDE, dtype=jnp.int32)
    groups = [[h * PLANE + i for i in range(PLANE)] for h in range(2)]

    def head_columns(array, head):
        return array[:, head * HEAD_SIZE : (head + 1) * HEAD_SIZE]

    def spread(sent):
        return lax.all_to_all(sent, "dp", 0, 0, axis_index_groups=groups)

    kv = jnp.stack(
        [
            jnp.concatenate([head_columns(keys, h), head_columns(values, h)], axis=1)
            for h in range(HEADS)
        ]
    )
    far = lax.ppermute(kv, AXES, route(0, 1, 0))
    pairs = lax.ppermute(block_pairs[0, :, 1].reshape(TILES, PICKS), AXES, route(-1, 0, 0))
    heads = (row + steps) & 3
    kv, *pieces = lax.optimization_barrier((kv, *split(heads, queries)))
    near_landed = spread(repeated(kv, 0))
    for turn in range(1, SIDE):
        pieces[turn] = lax.ppermute(pieces[turn], AXES, route(0, 0, turn))
    far_sent = repeated(far, 2 * 10**10)
    far_sent, near_landed, pieces[1], pieces[3] = lax.optimization_barrier(
        (far_sent, near_landed, pieces[1], pieces[3])
    )
    far_landed = spread(far_sent)

    blocks = half * PLANE + ((row - steps) & 3) * SIDE + column
    chosen = jnp.take(pairs, blocks, axis=0)
    slots = (chosen & 15) + ((chosen >> 4) ^ half) * PLANE
    back = [None] * SIDE
    for turns in ((1, 3), (2, 0)):
        mixed = attention(turns, slots, [pieces[turn] for turn in turns], near_landed, far_landed)
        for turn, rows in zip(turns, mixed):
            back[turn] = lax.ppermute(rows, AXES, route(1, 0, -turn))
        slots, mixed = lax.optimization_barrier((slots, mixed))
    return assemble(heads, back)[None]


def solution(mesh):
    placed = (
        P("pipe", "dp", None),
        P("pipe", "dp", None),
        P("pipe", "dp", None),
        P("pipe", None, None),
    )
    return jax.shard_map(
        on_device, mesh=mesh, in_specs=placed, out_specs=P("pipe", "dp", None), check_vma=False
    )
```
